32 devices in a mesh: batch: 2 (over y), expert: 16 (over z, x, core).
Axes of the slice: x: 2, y: 2, z: 4, core: 2. Of those that a mesh axis runs over, the one named last changes fastest.
Arguments:
- resid: bfloat16 [1024, 2048], P(('batch', 'expert')), may hold values from -6 to 6
- queries: bfloat16 [1024, 2048], P(('batch', 'expert')), may hold values from -6 to 6
- enc_keys: bfloat16 [32, 32, 2048], P(('batch', 'expert')), may hold values from -6 to 6
- enc_values: bfloat16 [32, 32, 2048], P(('batch', 'expert')), may hold values from -6 to 6
- src_lengths: int32 [32], P(('batch', 'expert')), may hold values from 2 to 32, as said below
- ln_gain: float32 [2048], replicated, may hold values from 0.5 to 1.5
- router: bfloat16 [2048, 16], replicated, may hold values from -0.125 to 0.125
- w_in: bfloat16 [16, 2048, 4096], P('expert', None, 'batch'), may hold values from -0.125 to 0.125
- w_out: bfloat16 [16, 4096, 2048], P('expert', 'batch'), may hold values from -0.09375 to 0.09375
- expert_ids: int32 [1024, 2], P(('batch', 'expert')), may hold values from 0 to 15, all different within a row; in each aligned block of 32 rows (0 to 31, 32 to 63, ...) at most 8 rows name the same one
Outputs:
- mixed: bfloat16 [1024, 2048], P(('batch', 'expert'))
The draws below stay inside these ranges and needn't reach their ends.
Inputs may be any that keep to these rules, and one draw needn't show every extreme that they name: `expert_ids`: each row names two different experts. In each aligned block of 32 rows (the rows of one device) no expert is named more than 8 times, a bound that some block reaches. `src_lengths`: some source sentence has all 32 positions valid.
All inputs are finite; a program needn't handle non-finite values.
Results may differ from the reference program's by a relative error of at most 0.005.
Values may be sent and summed in bfloat16 or wider, within the bound.
A program may use at most 64 MiB of HBM per device.

```python
import math
import jax
import jax.numpy as jnp
import numpy as np
from jax import lax

D = 2048
HEADS = 16
HEAD_DIM = 128
FF = 4096
LANGS = 32
SRC_LEN = 32
EXPERTS = 16
SRC = 32
ROWS = 1024
CAP = 8
N_BATCH = 2
N_EXPERT = 16


def draw_queries(key, part):
    noise = jnp.clip(jax.random.normal(jax.random.fold_in(key, 11), (ROWS, D), jnp.float32), -6.0, 6.0)
    return noise.astype(jnp.bfloat16)


def draw_enc_keys(key, part):
    noise = jnp.clip(jax.random.normal(jax.random.fold_in(key, 12), (SRC, SRC_LEN, D), jnp.float32), -6.0, 6.0)
    return noise.astype(jnp.bfloat16)


def draw_src_lengths(key, part):
    base = jax.random.fold_in(key, 13)
    first_key, second_key = jax.random.split(base)
    lengths = jax.random.randint(first_key, (SRC,), 2, SRC_LEN + 1)
    chosen_spot = jax.random.randint(second_key, (), 0, SRC)
    return lengths.at[chosen_spot].set(SRC_LEN).astype(jnp.int32)


def block_scale(stream_key, shape, cuts, least, largest):
    level = 1.0
    for axis_at, shards_of in cuts:
        draws = jax.random.uniform(jax.random.fold_in(jax.random.fold_in(stream_key, 6), axis_at), (shards_of,), jnp.float32, least / len(cuts), largest / len(cuts))
        level = level * jnp.repeat(jnp.exp(draws), shape[axis_at] // shards_of).reshape((-1,) + (1,) * (len(shape) - 1 - axis_at))
    return level


def assign_block(rng, own, number, rows, number_of, top, limit, skew):
    sequence = jax.random.permutation(rng, number_of)
    packed, ordinary = shares(number_of, rows * top, limit, skew, True), shares(number_of, rows * top, limit, skew, False)
    places = jnp.arange(number_of)

    def named(sizes, rotation):
        used = int((sizes > 0).sum())
        fixed = max(1, used // 4)
        passed = fixed + (places - fixed + rotation * (used - fixed)) % max(1, number_of - fixed)
        return jnp.zeros((number_of,), jnp.int32).at[sequence[jnp.where(places < fixed, places, passed)]].set(jnp.asarray(sizes, jnp.int32))

    sizes = jnp.where(number % 4 == 0, named(packed, number // 4), named(ordinary, number - number // 4 - 1))
    mixed = jax.random.permutation(jax.random.fold_in(own, 3), number_of)
    source_of, sink = mixed[0:number_of // 2 * 2:2], mixed[1:number_of // 2 * 2:2]
    room = jnp.minimum(sizes[source_of] - 1, limit - sizes[sink]) // 2
    room = jnp.where((source_of == sequence[0]) | (sink == sequence[0]) | (sizes[sink] == 0), 0, jnp.maximum(room, 0))
    passed = jax.random.randint(jax.random.fold_in(own, 4), (number_of // 2,), 0, 1 << 20) % (room + 1)
    sizes = sizes.at[source_of].add(-passed).at[sink].add(passed)
    items = jnp.searchsorted(jnp.cumsum(sizes), jnp.arange(rows * top), side="right").astype(jnp.int32)
    grid = items.reshape(top, rows).T
    grid = grid[jax.random.permutation(jax.random.fold_in(own, 1), rows)]
    rotation = jax.random.randint(jax.random.fold_in(own, 2), (rows, 1), 0, top)
    return jnp.take_along_axis(grid, (jnp.arange(top)[None, :] + rotation) % top, axis=1)


def shares(number_of, total, reach, lean, full):
    portions = [(1 << 20) // math.isqrt(rank ** lean) + 1 for rank in range(1, number_of + 1)]
    largest = reach if full else min(reach, max(-(-total // number_of), total * portions[0] // sum(portions)))
    least = 1 if total - largest >= number_of - 1 else 0
    given, rest = [largest] + [least] * (number_of - 1), total - largest - least * (number_of - 1)
    while rest > 0:
        movable = [i for i in range(1, number_of) if given[i] < largest] or [i for i in range(1, number_of) if given[i] < reach]
        whole, left = sum([portions[i] for i in movable]), rest
        for i in movable:
            more = min(reach - given[i], max(1, left * portions[i] // whole), rest)
            given[i] = given[i] + more
            rest = rest - more
    return np.array(given)


def gaussian(key, extent, deviation, most, cuts=(), kind=jnp.bfloat16):
    result = jax.random.normal(key, extent, jnp.float32) * deviation
    if len(cuts) > 0:
        result = block_scale(key, extent, cuts, -0.22, 0.18) * result
    return jnp.clip(result, min=-most, max=most).astype(kind)


def setup_inputs(seed: int = 0) -> dict:
    keys = jax.random.split(jax.random.key(seed), 11)
    resid = gaussian(keys[0], (ROWS, D), 1.0, 6.0, ((0, 32),))
    queries = draw_queries(jax.random.fold_in(keys[10], 71), 0)
    enc_keys = draw_enc_keys(jax.random.fold_in(keys[10], 71), 0)
    enc_values = gaussian(keys[3], (SRC, SRC_LEN, D), 1.0, 6.0, ((0, 32),))
    src_lengths = draw_src_lengths(jax.random.fold_in(keys[10], 71), 0)
    ln_gain = jnp.clip(1.0 + 0.1 * jax.random.normal(keys[5], (D,), jnp.float32), 0.5, 1.5)
    router = gaussian(keys[6], (D, EXPERTS), D ** -0.5, 0.125)
    w_in = gaussian(keys[7], (EXPERTS, D, FF), D ** -0.5, 0.125, ((0, 16), (2, 2)))
    w_out = gaussian(keys[8], (EXPERTS, FF, D), FF ** -0.5, 0.09375, ((0, 16), (1, 2)))
    expert_ids_keys = jax.random.split(jax.random.fold_in(keys[9], 1), ROWS // LANGS)
    expert_ids_turns = jax.random.permutation(jax.random.fold_in(keys[9], 3), ROWS // LANGS)
    expert_ids = jax.vmap(lambda own, number: assign_block(jax.random.fold_in(keys[9], 2), own, number, LANGS, EXPERTS, 2, CAP, 2))(expert_ids_keys, expert_ids_turns).reshape((ROWS, 2))
    return dict(resid=resid, queries=queries, enc_keys=enc_keys, enc_values=enc_values, src_lengths=src_lengths, ln_gain=ln_gain, router=router, w_in=w_in, w_out=w_out, expert_ids=expert_ids)


def attend_rows(resid, queries, enc_keys, enc_values, src_lengths, ln_gain):
    query_heads = queries.astype(jnp.float32).reshape(SRC, LANGS, HEADS, HEAD_DIM)
    key_heads = enc_keys.astype(jnp.float32).reshape(SRC, SRC_LEN, HEADS, HEAD_DIM)
    value_heads = enc_values.astype(jnp.float32).reshape(SRC, SRC_LEN, HEADS, HEAD_DIM)
    scores = jnp.einsum('slhd,sthd->shlt', query_heads, key_heads) / math.sqrt(HEAD_DIM)
    visible = jnp.arange(SRC_LEN, dtype=jnp.int32)[None, :] < src_lengths[:, None]
    scores = jnp.where(visible[:, None, None, :], scores, -1e+30)
    top_score = lax.optimization_barrier(jnp.max(scores, axis=-1, keepdims=True))
    powers = jnp.exp(scores - top_score)
    weights = (powers / lax.optimization_barrier(jnp.sum(powers, axis=-1, keepdims=True))).astype(jnp.bfloat16)
    context = jnp.einsum('shlt,sthd->slhd', weights.astype(jnp.float32), value_heads).reshape(ROWS, D)
    summed = resid.astype(jnp.float32) + context
    center = lax.optimization_barrier(jnp.mean(summed, axis=-1, keepdims=True))
    spread = lax.optimization_barrier(jnp.mean((summed - center) ** 2, axis=-1, keepdims=True))
    normed = ((summed - center) * lax.rsqrt(spread + 1e-05) * ln_gain).astype(jnp.bfloat16)
    return (summed, normed)

def expert_apply(operands):
    inputs, first_weight, second_weight = operands
    hidden = jnp.maximum(jnp.dot(inputs, first_weight, preferred_element_type=jnp.float32), 0.0).astype(jnp.bfloat16)
    blocks = hidden.astype(jnp.float32).reshape(inputs.shape[0], N_BATCH, FF // N_BATCH)
    seconds = second_weight.astype(jnp.float32).reshape(N_BATCH, FF // N_BATCH, D)
    partial_value = jnp.einsum('rbf,bfd->brd', blocks, seconds)
    rounded = lax.optimization_barrier(partial_value.astype(jnp.bfloat16)).astype(jnp.float32)
    return lax.optimization_barrier(jnp.sum(rounded, axis=0)).astype(jnp.bfloat16)

def reference(resid, queries, enc_keys, enc_values, src_lengths, ln_gain, router, w_in, w_out, expert_ids):
    summed, normed = attend_rows(resid, queries, enc_keys, enc_values, src_lengths, ln_gain)
    logits = jnp.dot(normed, router, preferred_element_type=jnp.float32)
    gates = jax.nn.sigmoid(jnp.take_along_axis(logits, expert_ids, axis=1))
    devices_all = N_BATCH * N_EXPERT
    block_ids = expert_ids.reshape(devices_all, LANGS * 2)
    onehot = (block_ids[:, :, None] == jnp.arange(EXPERTS, dtype=jnp.int32)[None, None, :]).astype(jnp.int32)
    before = jnp.cumsum(onehot, axis=1) - onehot
    slots = lax.optimization_barrier(jnp.sum(before * onehot, axis=-1))
    owner = jnp.arange(devices_all, dtype=jnp.int32)[:, None] * CAP + slots
    flat_owner = owner.reshape(-1).astype(jnp.int32)
    flat_expert = expert_ids.reshape(-1).astype(jnp.int32)
    assigned = jnp.repeat(normed, 2, axis=0)
    buffers = jnp.zeros((EXPERTS, devices_all * CAP, D), jnp.bfloat16).at[flat_expert, flat_owner].set(assigned)
    results = lax.map(expert_apply, (buffers, w_in, w_out))
    returned = results[flat_expert, flat_owner].astype(jnp.float32).reshape(ROWS, 2, D)
    mixed = summed + lax.optimization_barrier(jnp.sum(gates[:, :, None] * returned, axis=1))
    return mixed.astype(jnp.bfloat16)
```

```python
import functools
import math

import jax
import jax.numpy as jnp
from jax import lax
from jax.experimental import pallas as pl
from jax.experimental.pallas import tpu as pltpu
from jax.sharding import PartitionSpec as P

D = 2048
HEADS = 16
HEAD_DIM = 128


def expert_term(inputs, first_weight, second_weight):
    hidden = jnp.maximum(
        jnp.dot(inputs, first_weight, preferred_element_type=jnp.float32), 0.0
    ).astype(jnp.bfloat16)
    return jnp.dot(hidden, second_weight, preferred_element_type=jnp.float32)


def on_device(
    resid, queries, enc_keys, enc_values, src_lengths, ln_gain, router, w_in, w_out, expert_ids
):
    row_count = resid.shape[0]
    key_count = enc_keys.shape[1]
    query_heads = queries.reshape(row_count, HEADS, HEAD_DIM)
    key_heads = enc_keys.reshape(key_count, HEADS, HEAD_DIM)
    value_heads = enc_values.reshape(key_count, HEADS, HEAD_DIM)
    scores = jnp.einsum(
        "rhd,thd->hrt", query_heads, key_heads, preferred_element_type=jnp.float32
    ) / math.sqrt(HEAD_DIM)
    visible = jnp.arange(key_count, dtype=jnp.int32) < src_lengths[0]
    scores = jnp.where(visible[None, None, :], scores, -1e30)
    top_score = jnp.max(scores, axis=-1, keepdims=True)
    powers = jnp.exp(scores - top_score)
    weights = (powers / jnp.sum(powers, axis=-1, keepdims=True)).astype(jnp.bfloat16)
    context = jnp.einsum(
        "hrt,thd->rhd", weights, value_heads, preferred_element_type=jnp.float32
    ).reshape(row_count, D)
    summed = resid.astype(jnp.float32) + context
    center = jnp.mean(summed, axis=-1, keepdims=True)
    spread = jnp.mean((summed - center) ** 2, axis=-1, keepdims=True)
    normed = ((summed - center) * lax.rsqrt(spread + 1e-05) * ln_gain).astype(jnp.bfloat16)
    experts_all = router.shape[1]
    capacity = max(2, 4 * row_count // experts_all)
    logits = jnp.dot(normed, router, preferred_element_type=jnp.float32)
    flat_expert = expert_ids.reshape(-1)
    onehot = (flat_expert[:, None] == jnp.arange(experts_all, dtype=jnp.int32)[None, :]).astype(
        jnp.int32
    )
    earlier = jnp.tri(flat_expert.shape[0], k=-1, dtype=jnp.bfloat16)
    before = jnp.dot(
        earlier, onehot.astype(jnp.bfloat16), preferred_element_type=jnp.float32
    ).astype(jnp.int32)
    slots = jnp.sum(before * onehot, axis=1)
    flat_owner = flat_expert * capacity + slots
    chosen = jnp.sum(
        onehot.reshape(row_count, 2, experts_all).astype(jnp.float32) * logits[:, None, :], axis=-1
    )
    gates = jax.nn.sigmoid(chosen)
    assigned = jnp.repeat(normed, 2, axis=0)
    outgoing = jnp.zeros((experts_all * capacity, D), jnp.bfloat16).at[flat_owner].set(assigned)
    outgoing = outgoing.reshape(experts_all, capacity, D)
    first_weight = w_in[0]
    second_weight = w_out[0]
    stacked = lax.all_gather(outgoing[:, None], "batch", axis=1, tiled=True)
    arrived = lax.all_to_all(stacked, "expert", split_axis=0, concat_axis=0, tiled=True)
    sources = arrived.shape[0]
    item_count = arrived.shape[1]
    partial_value = expert_term(arrived.reshape(-1, D), first_weight, second_weight)
    outbound = partial_value.astype(jnp.bfloat16).reshape(sources, item_count, capacity, D)
    returned_parts = lax.all_to_all(outbound, "expert", split_axis=0, concat_axis=0, tiled=True)
    totals = lax.psum_scatter(
        returned_parts.astype(jnp.float32).astype(jnp.bfloat16),
        "batch",
        scatter_dimension=1,
        tiled=True,
    )
    expert_out = totals.reshape(experts_all * capacity, D)
    returned = jnp.take(expert_out, flat_owner, axis=0).astype(jnp.float32).reshape(row_count, 2, D)
    mixed = summed + jnp.sum(gates[:, :, None] * returned, axis=1)
    return mixed.astype(jnp.bfloat16)


GROUPS = 2
STRIDE = 5
TILE_ONE = 256
TILE_TWO = 512
PIECES = 4


def fused_kernel(
    experts,
    cap,
    resid_ref,
    queries_ref,
    keys_ref,
    values_ref,
    length_ref,
    gain_ref,
    router_ref,
    ids_ref,
    first_hbm,
    second_hbm,
    out_ref,
    first,
    second,
    slots,
    arrived,
    block,
    hidden,
    mine,
    sent,
    taken,
    back,
    returned,
    summed,
    context,
    first_sem,
    second_sem,
    out_send,
    out_recv,
    fwd_send,
    fwd_recv,
    sum_send,
    sum_recv,
    ret_send,
    ret_recv,
):
    b = lax.axis_index("batch")
    e = lax.axis_index("expert")
    mesh_id = pl.DeviceIdType.MESH
    rows = resid_ref.shape[0]
    width = resid_ref.shape[1]
    units = first.shape[1]
    per = experts // GROUPS
    piece = width // PIECES
    unit_piece = units // PIECES
    tiles_two = width // TILE_TWO
    peer = 1 - b

    def ahead(k):
        return lax.rem(e + STRIDE * k, experts)

    def behind(k):
        return lax.rem(e + STRIDE * experts - STRIDE * k, experts)

    barrier = pltpu.get_barrier_semaphore()

    @pl.loop(1, experts)
    def _(k):
        pl.semaphore_signal(barrier, inc=1, device_id=(b, ahead(k)), device_id_type=mesh_id)

    pl.semaphore_signal(barrier, inc=1, device_id=(peer, e), device_id_type=mesh_id)

    def first_copy(p):
        part = pl.ds(p * piece, piece)
        return pltpu.make_async_copy(first_hbm.at[0, part, :], first.at[part, :], first_sem.at[p])

    def second_copy(p):
        part = pl.ds(p * unit_piece, unit_piece)
        return pltpu.make_async_copy(
            second_hbm.at[0, part, :], second.at[part, :], second_sem.at[p]
        )

    for p in range(PIECES):
        first_copy(p).start()
    for p in range(PIECES):
        second_copy(p).start()

    tokens = keys_ref.shape[1]
    parts = []
    for h in range(HEADS):
        lanes = slice(h * HEAD_DIM, (h + 1) * HEAD_DIM)
        parts.append(
            lax.dot_general(
                queries_ref[:, lanes],
                keys_ref[0, :, lanes],
                (((1,), (1,)), ((), ())),
                preferred_element_type=jnp.float32,
            )
        )
    scores = jnp.concatenate(parts, axis=0) / math.sqrt(HEAD_DIM)
    visible = lax.broadcasted_iota(jnp.int32, scores.shape, 1) < length_ref[0]
    scores = jnp.where(visible, scores, -1e30)
    powers = jnp.exp(scores - jnp.max(scores, axis=-1, keepdims=True))
    weights = (powers / jnp.sum(powers, axis=-1, keepdims=True)).astype(jnp.bfloat16)
    for h in range(HEADS):
        lanes = slice(h * HEAD_DIM, (h + 1) * HEAD_DIM)
        context[:, lanes] = jnp.dot(
            weights[h * rows : (h + 1) * rows, :],
            values_ref[0, :, lanes],
            preferred_element_type=jnp.float32,
        )
    total = resid_ref[...].astype(jnp.float32) + context[...]
    summed[...] = total
    center = jnp.mean(total, axis=-1, keepdims=True)
    spread = jnp.mean((total - center) ** 2, axis=-1, keepdims=True)
    normed = ((total - center) * lax.rsqrt(spread + 1e-05) * gain_ref[...]).astype(jnp.bfloat16)

    count = experts * cap
    column = lax.broadcasted_iota(jnp.int32, (rows, count), 1)
    column_expert = lax.div(column, cap)
    column_slot = lax.rem(column, cap).astype(jnp.float32)
    named_0 = (ids_ref[:, 0:1] == column_expert).astype(jnp.float32)
    named_1 = (ids_ref[:, 1:2] == column_expert).astype(jnp.float32)
    earlier = (
        lax.broadcasted_iota(jnp.int32, (rows, rows), 1)
        < lax.broadcasted_iota(jnp.int32, (rows, rows), 0)
    ).astype(jnp.bfloat16)
    before = jnp.dot(
        earlier, (named_0 + named_1).astype(jnp.bfloat16), preferred_element_type=jnp.float32
    )
    here = (before == column_slot).astype(jnp.float32)
    place_0 = named_0 * here
    place_1 = named_1 * here
    filled = lax.dot_general(
        (place_0 + place_1).astype(jnp.bfloat16),
        normed,
        (((0,), (0,)), ((), ())),
        preferred_element_type=jnp.float32,
    )
    slots[...] = filled.reshape(experts, cap, width).astype(jnp.bfloat16)

    def dispatch(k, target, at):
        return pltpu.make_async_remote_copy(
            src_ref=slots.at[target],
            dst_ref=arrived.at[0, at],
            send_sem=out_send.at[k],
            recv_sem=out_recv.at[k],
            device_id=(b, target),
            device_id_type=mesh_id,
        )

    def forward(k):
        return pltpu.make_async_remote_copy(
            src_ref=arrived.at[0, k],
            dst_ref=arrived.at[1, k],
            send_sem=fwd_send.at[k],
            recv_sem=fwd_recv.at[k],
            device_id=(peer, e),
            device_id_type=mesh_id,
        )

    def partial_copy(g, t):
        part = (pl.ds(g * per, per), slice(None), pl.ds(t * TILE_TWO, TILE_TWO))
        return pltpu.make_async_remote_copy(
            src_ref=sent.at[part],
            dst_ref=taken.at[part],
            send_sem=sum_send.at[g, t],
            recv_sem=sum_recv.at[g, t],
            device_id=(peer, e),
            device_id_type=mesh_id,
        )

    def give_back(k, target, at):
        return pltpu.make_async_remote_copy(
            src_ref=back.at[k],
            dst_ref=returned.at[at],
            send_sem=ret_send.at[k],
            recv_sem=ret_recv.at[k],
            device_id=(b, target),
            device_id_type=mesh_id,
        )

    pl.semaphore_wait(barrier, experts)

    @pl.loop(1, experts)
    def _(k):
        dispatch(k, ahead(k), k).start()

    arrived[0, 0] = slots[e]
    forward(0).start()

    logits = jnp.dot(normed, router_ref[...], preferred_element_type=jnp.float32)
    lane = lax.broadcasted_iota(jnp.int32, logits.shape, 1)
    gate_0 = jax.nn.sigmoid(
        jnp.sum(jnp.where(ids_ref[:, 0:1] == lane, logits, 0.0), axis=-1, keepdims=True)
    )
    gate_1 = jax.nn.sigmoid(
        jnp.sum(jnp.where(ids_ref[:, 1:2] == lane, logits, 0.0), axis=-1, keepdims=True)
    )

    def pass_on(k):
        dispatch(k, ahead(k), k).wait_recv()
        forward(k).start()

    def gather(g):
        half = per * cap
        for side in range(2):
            block[side * half : (side + 1) * half, :] = (
                arrived[side, g * per : (g + 1) * per]
                .astype(jnp.float32)
                .reshape(half, width)
                .astype(jnp.bfloat16)
            )

    def into_hidden(g):
        @pl.loop(0, units // TILE_ONE)
        def _(t):
            lanes = pl.ds(pl.multiple_of(t * TILE_ONE, TILE_ONE), TILE_ONE)
            hidden[:, lanes] = jnp.maximum(
                jnp.dot(block[...], first[:, lanes], preferred_element_type=jnp.float32), 0.0
            ).astype(jnp.bfloat16)
            if g + 1 < GROUPS:
                pass_on((g + 1) * per + t)

    def out_of_hidden(g):
        half = per * cap
        group = pl.ds(g * per, per)

        @pl.loop(0, tiles_two)
        def _(t):
            lanes = pl.ds(pl.multiple_of(t * TILE_TWO, TILE_TWO), TILE_TWO)
            result = jnp.dot(hidden[...], second[:, lanes], preferred_element_type=jnp.float32)
            sent[group, :, lanes] = (
                result[half:, :].reshape(per, cap, TILE_TWO).astype(jnp.bfloat16)
            )
            partial_copy(g, t).start()
            mine[group, :, lanes] = (
                result[:half, :].reshape(per, cap, TILE_TWO).astype(jnp.bfloat16)
            )

    def finish(g):
        @pl.loop(0, tiles_two)
        def _(t):
            partial_copy(g, t).wait_recv()

        def add(k):
            return (mine[k].astype(jnp.float32) + taken[k].astype(jnp.float32)).astype(
                jnp.bfloat16
            )

        if g == 0:
            returned[e] = add(0)

        @pl.loop(1 if g == 0 else g * per, (g + 1) * per)
        def _(k):
            back[k] = add(k)
            give_back(k, behind(k), e).start()

    @pl.loop(1, per)
    def _(k):
        pass_on(k)

    for g in range(GROUPS):

        @pl.loop(g * per, (g + 1) * per)
        def _(k):
            forward(k).wait_recv()

        if g == 0:
            for p in range(PIECES):
                first_copy(p).wait()
        gather(g)
        into_hidden(g)
        if g == 0:
            for p in range(PIECES):
                second_copy(p).wait()
        if g > 0:
            finish(g - 1)
        out_of_hidden(g)
    finish(GROUPS - 1)

    @pl.loop(1, experts)
    def _(k):
        give_back(k, behind(k), ahead(k)).wait_recv()

    answers = returned[...].astype(jnp.float32).reshape(count, width).astype(jnp.bfloat16)
    chosen_0 = jnp.dot(
        place_0.astype(jnp.bfloat16), answers, preferred_element_type=jnp.float32
    )
    chosen_1 = jnp.dot(
        place_1.astype(jnp.bfloat16), answers, preferred_element_type=jnp.float32
    )
    out_ref[...] = (summed[...] + (gate_0 * chosen_0 + gate_1 * chosen_1)).astype(out_ref.dtype)

    @pl.loop(1, experts)
    def _(k):
        dispatch(k, ahead(k), k).wait_send()
        give_back(k, behind(k), e).wait_send()

    @pl.loop(0, experts)
    def _(k):
        forward(k).wait_send()

    for g in range(GROUPS):

        @pl.loop(0, tiles_two)
        def _(t):
            partial_copy(g, t).wait_send()


def fused(*arrays):
    resid, router, w_in, w_out = arrays[0], arrays[6], arrays[7], arrays[8]
    row_count, width = resid.shape
    experts = router.shape[1]
    cap = max(2, 4 * row_count // experts)
    units = w_in.shape[2]
    per = experts // GROUPS
    tiles_two = width // TILE_TWO
    bf16, f32 = jnp.bfloat16, jnp.float32
    dma = pltpu.SemaphoreType.DMA
    vmem = pl.BlockSpec(memory_space=pltpu.VMEM)
    smem = pl.BlockSpec(memory_space=pltpu.SMEM)
    hbm = pl.BlockSpec(memory_space=pl.ANY)
    operands = (*arrays[:5], arrays[5].reshape(1, width), router, arrays[9], w_in, w_out)
    return pl.pallas_call(
        functools.partial(fused_kernel, experts, cap),
        out_shape=jax.ShapeDtypeStruct((row_count, width), bf16),
        in_specs=[vmem, vmem, vmem, vmem, smem, vmem, vmem, vmem, hbm, hbm],
        out_specs=vmem,
        scratch_shapes=[
            pltpu.VMEM((width, units), bf16),
            pltpu.VMEM((units, width), bf16),
            pltpu.VMEM((experts, cap, width), bf16),
            pltpu.VMEM((2, experts, cap, width), bf16),
            pltpu.VMEM((2 * per * cap, width), bf16),
            pltpu.VMEM((2 * per * cap, units), bf16),
            pltpu.VMEM((experts, cap, width), bf16),
            pltpu.VMEM((experts, cap, width), bf16),
            pltpu.VMEM((experts, cap, width), bf16),
            pltpu.VMEM((experts, cap, width), bf16),
            pltpu.VMEM((experts, cap, width), bf16),
            pltpu.VMEM((row_count, width), f32),
            pltpu.VMEM((row_count, width), f32),
            dma((PIECES,)),
            dma((PIECES,)),
            dma((experts,)),
            dma((experts,)),
            dma((experts,)),
            dma((experts,)),
            dma((GROUPS, tiles_two)),
            dma((GROUPS, tiles_two)),
            dma((experts,)),
            dma((experts,)),
        ],
        compiler_params=pltpu.CompilerParams(
            collective_id=0, has_side_effects=True, vmem_limit_bytes=50 * 2**20
        ),
    )(*operands)


def per_device(mesh, *arrays):
    row_count = arrays[0].shape[0]
    experts = mesh.shape["expert"]
    cap = max(2, 4 * row_count // arrays[6].shape[1])
    if mesh.shape["batch"] == 2 and arrays[6].shape[1] == experts and cap == 8 and experts == 16:
        return fused(*arrays)
    return on_device(*arrays)


def solution(mesh):
    return jax.shard_map(
        functools.partial(per_device, mesh),
        mesh=mesh,
        in_specs=(
            P(("batch", "expert"), None),
            P(("batch", "expert"), None),
            P(("batch", "expert"), None, None),
            P(("batch", "expert"), None, None),
            P(("batch", "expert")),
            P(),
            P(),
            P("expert", None, "batch"),
            P("expert", "batch", None),
            P(("batch", "expert"), None),
        ),
        out_specs=P(("batch", "expert"), None),
        check_vma=False,
    )
```

```python
import functools
import math

import jax
import jax.numpy as jnp
from jax import lax
from jax.experimental import pallas as pl
from jax.experimental.pallas import tpu as pltpu
from jax.sharding import PartitionSpec as P

D = 2048
HEADS = 16
HEAD_DIM = 128


def expert_term(inputs, first_weight, second_weight):
    hidden = jnp.maximum(
        jnp.dot(inputs, first_weight, preferred_element_type=jnp.float32), 0.0
    ).astype(jnp.bfloat16)
    return jnp.dot(hidden, second_weight, preferred_element_type=jnp.float32)


def on_device(
    resid, queries, enc_keys, enc_values, src_lengths, ln_gain, router, w_in, w_out, expert_ids
):
    row_count = resid.shape[0]
    key_count = enc_keys.shape[1]
    query_heads = queries.reshape(row_count, HEADS, HEAD_DIM)
    key_heads = enc_keys.reshape(key_count, HEADS, HEAD_DIM)
    value_heads = enc_values.reshape(key_count, HEADS, HEAD_DIM)
    scores = jnp.einsum(
        "rhd,thd->hrt", query_heads, key_heads, preferred_element_type=jnp.float32
    ) / math.sqrt(HEAD_DIM)
    visible = jnp.arange(key_count, dtype=jnp.int32) < src_lengths[0]
    scores = jnp.where(visible[None, None, :], scores, -1e30)
    top_score = jnp.max(scores, axis=-1, keepdims=True)
    powers = jnp.exp(scores - top_score)
    weights = (powers / jnp.sum(powers, axis=-1, keepdims=True)).astype(jnp.bfloat16)
    context = jnp.einsum(
        "hrt,thd->rhd", weights, value_heads, preferred_element_type=jnp.float32
    ).reshape(row_count, D)
    summed = resid.astype(jnp.float32) + context
    center = jnp.mean(summed, axis=-1, keepdims=True)
    spread = jnp.mean((summed - center) ** 2, axis=-1, keepdims=True)
    normed = ((summed - center) * lax.rsqrt(spread + 1e-05) * ln_gain).astype(jnp.bfloat16)
    experts_all = router.shape[1]
    capacity = max(2, 4 * row_count // experts_all)
    logits = jnp.dot(normed, router, preferred_element_type=jnp.float32)
    flat_expert = expert_ids.reshape(-1)
    onehot = (flat_expert[:, None] == jnp.arange(experts_all, dtype=jnp.int32)[None, :]).astype(
        jnp.int32
    )
    earlier = jnp.tri(flat_expert.shape[0], k=-1, dtype=jnp.bfloat16)
    before = jnp.dot(
        earlier, onehot.astype(jnp.bfloat16), preferred_element_type=jnp.float32
    ).astype(jnp.int32)
    slots = jnp.sum(before * onehot, axis=1)
    flat_owner = flat_expert * capacity + slots
    chosen = jnp.sum(
        onehot.reshape(row_count, 2, experts_all).astype(jnp.float32) * logits[:, None, :], axis=-1
    )
    gates = jax.nn.sigmoid(chosen)
    assigned = jnp.repeat(normed, 2, axis=0)
    outgoing = jnp.zeros((experts_all * capacity, D), jnp.bfloat16).at[flat_owner].set(assigned)
    outgoing = outgoing.reshape(experts_all, capacity, D)
    first_weight = w_in[0]
    second_weight = w_out[0]
    stacked = lax.all_gather(outgoing[:, None], "batch", axis=1, tiled=True)
    arrived = lax.all_to_all(stacked, "expert", split_axis=0, concat_axis=0, tiled=True)
    sources = arrived.shape[0]
    item_count = arrived.shape[1]
    partial_value = expert_term(arrived.reshape(-1, D), first_weight, second_weight)
    outbound = partial_value.astype(jnp.bfloat16).reshape(sources, item_count, capacity, D)
    returned_parts = lax.all_to_all(outbound, "expert", split_axis=0, concat_axis=0, tiled=True)
    totals = lax.psum_scatter(
        returned_parts.astype(jnp.float32).astype(jnp.bfloat16),
        "batch",
        scatter_dimension=1,
        tiled=True,
    )
    expert_out = totals.reshape(experts_all * capacity, D)
    returned = jnp.take(expert_out, flat_owner, axis=0).astype(jnp.float32).reshape(row_count, 2, D)
    mixed = summed + jnp.sum(gates[:, :, None] * returned, axis=1)
    return mixed.astype(jnp.bfloat16)


PLANES = 4
ORDER = (0, 2, 1, 3)
GROUPS = len(ORDER)
LAG = 2
TILE_ONE = 512
TILE_TWO = 512
PIECES = 4


def fused_kernel(
    experts,
    cap,
    length_ref,
    resid_hbm,
    queries_hbm,
    keys_hbm,
    values_hbm,
    gain_hbm,
    router_hbm,
    ids_hbm,
    first_hbm,
    second_hbm,
    out_ref,
    first,
    second,
    slots,
    arrived,
    block,
    hidden,
    mine,
    sent,
    taken,
    back,
    returned,
    summed,
    context,
    resid_ref,
    queries_ref,
    keys_ref,
    values_ref,
    gain_ref,
    router_ref,
    ids_ref,
    input_sem,
    first_sem,
    second_sem,
    out_send,
    out_recv,
    fwd_send,
    fwd_recv,
    sum_send,
    sum_recv,
    ret_send,
    ret_recv,
):
    b = lax.axis_index("batch")
    e = lax.axis_index("expert")
    mesh_id = pl.DeviceIdType.MESH
    rows = resid_ref.shape[0]
    width = resid_ref.shape[1]
    units = first.shape[1]
    per = experts // GROUPS
    piece = width // PIECES
    unit_piece = units // PIECES
    tiles_two = width // TILE_TWO
    peer = 1 - b

    plane = lax.div(e, per)
    spot = lax.rem(e, per)

    def ahead(g, j):
        return lax.rem(plane + ORDER[g], PLANES) * per + lax.rem(spot + j, per)

    def behind(g, j):
        return lax.rem(plane + PLANES - ORDER[g], PLANES) * per + lax.rem(spot + per - j, per)

    barrier = pltpu.get_barrier_semaphore()

    for g in range(GROUPS):

        @pl.loop(1 if g == 0 else 0, per)
        def _(j):
            pl.semaphore_signal(
                barrier, inc=1, device_id=(b, ahead(g, j)), device_id_type=mesh_id
            )

    pl.semaphore_signal(barrier, inc=1, device_id=(peer, e), device_id_type=mesh_id)

    inputs = [
        pltpu.make_async_copy(source, target, input_sem.at[i])
        for i, (source, target) in enumerate(
            (
                (queries_hbm, queries_ref),
                (keys_hbm, keys_ref),
                (values_hbm, values_ref),
                (resid_hbm, resid_ref),
                (gain_hbm, gain_ref),
                (ids_hbm, ids_ref),
                (router_hbm, router_ref),
            )
        )
    ]
    for copy in inputs:
        copy.start()

    def first_copy(p):
        part = pl.ds(p * piece, piece)
        return pltpu.make_async_copy(first_hbm.at[0, part, :], first.at[part, :], first_sem.at[p])

    def second_copy(p):
        part = pl.ds(p * unit_piece, unit_piece)
        return pltpu.make_async_copy(
            second_hbm.at[0, part, :], second.at[part, :], second_sem.at[p]
        )

    for p in range(PIECES):
        first_copy(p).start()
    for p in range(PIECES):
        second_copy(p).start()

    for copy in inputs:
        copy.wait()

    parts = []
    for h in range(HEADS):
        lanes = slice(h * HEAD_DIM, (h + 1) * HEAD_DIM)
        parts.append(
            lax.dot_general(
                queries_ref[:, lanes],
                keys_ref[0, :, lanes],
                (((1,), (1,)), ((), ())),
                preferred_element_type=jnp.float32,
            )
        )
    scores = jnp.concatenate(parts, axis=0) / math.sqrt(HEAD_DIM)
    visible = lax.broadcasted_iota(jnp.int32, scores.shape, 1) < length_ref[0]
    scores = jnp.where(visible, scores, -1e30)
    powers = jnp.exp(scores - jnp.max(scores, axis=-1, keepdims=True))
    weights = (powers / jnp.sum(powers, axis=-1, keepdims=True)).astype(jnp.bfloat16)
    for h in range(HEADS):
        lanes = slice(h * HEAD_DIM, (h + 1) * HEAD_DIM)
        context[:, lanes] = jnp.dot(
            weights[h * rows : (h + 1) * rows, :],
            values_ref[0, :, lanes],
            preferred_element_type=jnp.float32,
        )
    total = resid_ref[...].astype(jnp.float32) + context[...]
    summed[...] = total
    center = jnp.mean(total, axis=-1, keepdims=True)
    spread = jnp.mean((total - center) ** 2, axis=-1, keepdims=True)
    normed = ((total - center) * lax.rsqrt(spread + 1e-05) * gain_ref[...]).astype(jnp.bfloat16)

    count = experts * cap
    bf16 = jnp.bfloat16

    def product(left, right, left_axis, right_axis):
        return lax.dot_general(
            left.astype(bf16),
            right.astype(bf16),
            (((left_axis,), (right_axis,)), ((), ())),
            preferred_element_type=jnp.float32,
        )

    line = lax.broadcasted_iota(jnp.int32, (count, rows), 0)
    line_expert = lax.div(line, cap)
    line_slot = lax.rem(line, cap).astype(jnp.float32)
    named_0 = (ids_ref[0:1, :] == line_expert).astype(jnp.float32)
    named_1 = (ids_ref[1:2, :] == line_expert).astype(jnp.float32)
    row_from = lax.broadcasted_iota(jnp.int32, (rows, rows), 0)
    row_to = lax.broadcasted_iota(jnp.int32, (rows, rows), 1)
    before = product(named_0 + named_1, (row_from < row_to).astype(jnp.float32), 1, 0)
    here = (before == line_slot).astype(jnp.float32)
    place_0 = named_0 * here
    place_1 = named_1 * here
    filled = product(place_0 + place_1, normed, 1, 0)
    slots[...] = filled.reshape(experts, cap, width).astype(jnp.bfloat16)

    def dispatch(g, j):
        k = g * per + j
        return pltpu.make_async_remote_copy(
            src_ref=slots.at[ahead(g, j)],
            dst_ref=arrived.at[0, k],
            send_sem=out_send.at[k],
            recv_sem=out_recv.at[k],
            device_id=(b, ahead(g, j)),
            device_id_type=mesh_id,
        )

    def forward(k):
        return pltpu.make_async_remote_copy(
            src_ref=arrived.at[0, k],
            dst_ref=arrived.at[1, k],
            send_sem=fwd_send.at[k],
            recv_sem=fwd_recv.at[k],
            device_id=(peer, e),
            device_id_type=mesh_id,
        )

    def partial_copy(g, t):
        part = (pl.ds(g * per, per), slice(None), pl.ds(t * TILE_TWO, TILE_TWO))
        return pltpu.make_async_remote_copy(
            src_ref=sent.at[part],
            dst_ref=taken.at[part],
            send_sem=sum_send.at[g, t],
            recv_sem=sum_recv.at[g, t],
            device_id=(peer, e),
            device_id_type=mesh_id,
        )

    def give_back(g, j, at):
        k = g * per + j
        return pltpu.make_async_remote_copy(
            src_ref=back.at[k],
            dst_ref=returned.at[at],
            send_sem=ret_send.at[k],
            recv_sem=ret_recv.at[k],
            device_id=(b, behind(g, j)),
            device_id_type=mesh_id,
        )

    pl.semaphore_wait(barrier, experts)

    for g in range(2):

        @pl.loop(1 if g == 0 else 0, per)
        def _(j):
            dispatch(g, j).start()

    arrived[0, 0] = slots[e]
    forward(0).start()

    logits = product(normed, router_ref[...], 1, 1)
    number = lax.broadcasted_iota(jnp.int32, (experts, rows), 0)
    unit = (row_from == row_to).astype(jnp.float32)

    def gate(at):
        named = (ids_ref[at : at + 1, :] == number).astype(jnp.float32)
        turned = product(unit, named, 1, 1)
        return jax.nn.sigmoid(jnp.sum(turned * logits, axis=-1, keepdims=True))

    gate_0 = gate(0)
    gate_1 = gate(1)

    def pass_on(g, j):
        dispatch(g, j).wait_recv()
        forward(g * per + j).start()
        if 1 <= g < GROUPS - 1:
            dispatch(g + 1, j).start()

    def gather(g):
        half = per * cap
        for side in range(2):
            block[side * half : (side + 1) * half, :] = (
                arrived[side, g * per : (g + 1) * per]
                .astype(jnp.float32)
                .reshape(half, width)
                .astype(jnp.bfloat16)
            )

    def into_hidden(g):
        @pl.loop(0, units // TILE_ONE)
        def _(t):
            lanes = pl.ds(pl.multiple_of(t * TILE_ONE, TILE_ONE), TILE_ONE)
            hidden[:, lanes] = jnp.maximum(
                jnp.dot(block[...], first[:, lanes], preferred_element_type=jnp.float32), 0.0
            ).astype(jnp.bfloat16)
            if g + 2 < GROUPS:
                pass_on(g + 2, t)

    def out_of_hidden(g):
        half = per * cap
        group = pl.ds(g * per, per)

        @pl.loop(0, tiles_two)
        def _(t):
            lanes = pl.ds(pl.multiple_of(t * TILE_TWO, TILE_TWO), TILE_TWO)
            result = jnp.dot(hidden[...], second[:, lanes], preferred_element_type=jnp.float32)
            sent[group, :, lanes] = (
                result[half:, :].reshape(per, cap, TILE_TWO).astype(jnp.bfloat16)
            )
            partial_copy(g, t).start()
            mine[group, :, lanes] = (
                result[:half, :].reshape(per, cap, TILE_TWO).astype(jnp.bfloat16)
            )
            if g >= LAG:

                @pl.when(t == 0)
                def _():
                    await_partials(g - LAG)

                finish(g - LAG, t)

    def await_partials(g):
        @pl.loop(0, tiles_two)
        def _(t):
            partial_copy(g, t).wait_recv()

    def finish(g, j):
        k = g * per + j
        both = (mine[k].astype(jnp.float32) + taken[k].astype(jnp.float32)).astype(jnp.bfloat16)
        if g > 0:
            back[k] = both
            give_back(g, j, e).start()
        else:

            @pl.when(j == 0)
            def _():
                returned[e] = both

            @pl.when(j > 0)
            def _():
                back[k] = both
                give_back(g, j, e).start()

    @pl.loop(1, per)
    def _(j):
        pass_on(0, j)

    @pl.loop(0, per)
    def _(j):
        pass_on(1, j)

    for g in range(GROUPS):

        @pl.loop(g * per, (g + 1) * per)
        def _(k):
            forward(k).wait_recv()

        if g == 0:
            for p in range(PIECES):
                first_copy(p).wait()
        gather(g)
        into_hidden(g)
        if g == 0:
            for p in range(PIECES):
                second_copy(p).wait()
        out_of_hidden(g)
    for g in range(GROUPS - LAG, GROUPS):
        await_partials(g)

        @pl.loop(0, per)
        def _(j):
            finish(g, j)

    for g in range(GROUPS):

        @pl.loop(1 if g == 0 else 0, per)
        def _(j):
            give_back(g, j, ahead(g, j)).wait_recv()

    answers = returned[...].astype(jnp.float32).reshape(count, width).astype(jnp.bfloat16)
    chosen_0 = product(place_0, answers, 0, 0)
    chosen_1 = product(place_1, answers, 0, 0)
    out_ref[...] = (summed[...] + (gate_0 * chosen_0 + gate_1 * chosen_1)).astype(out_ref.dtype)

    for g in range(GROUPS):

        @pl.loop(1 if g == 0 else 0, per)
        def _(j):
            dispatch(g, j).wait_send()
            give_back(g, j, e).wait_send()

    @pl.loop(0, experts)
    def _(k):
        forward(k).wait_send()

    for g in range(GROUPS):

        @pl.loop(0, tiles_two)
        def _(t):
            partial_copy(g, t).wait_send()


def fused(*arrays):
    resid, router, w_in, w_out = arrays[0], arrays[6], arrays[7], arrays[8]
    row_count, width = resid.shape
    experts = router.shape[1]
    cap = max(2, 4 * row_count // experts)
    units = w_in.shape[2]
    per = experts // GROUPS
    tiles_two = width // TILE_TWO
    bf16, f32 = jnp.bfloat16, jnp.float32
    dma = pltpu.SemaphoreType.DMA
    vmem = pl.BlockSpec(memory_space=pltpu.VMEM)
    smem = pl.BlockSpec(memory_space=pltpu.SMEM)
    hbm = pl.BlockSpec(memory_space=pltpu.HBM)
    small = (*arrays[:4], arrays[5].reshape(1, width), router.T, arrays[9].T)
    operands = (arrays[4], *small, w_in, w_out)
    return pl.pallas_call(
        functools.partial(fused_kernel, experts, cap),
        out_shape=jax.ShapeDtypeStruct((row_count, width), bf16),
        in_specs=[smem] + [hbm] * 9,
        out_specs=vmem,
        scratch_shapes=[
            pltpu.VMEM((width, units), bf16),
            pltpu.VMEM((units, width), bf16),
            pltpu.VMEM((experts, cap, width), bf16),
            pltpu.VMEM((2, experts, cap, width), bf16),
            pltpu.VMEM((2 * per * cap, width), bf16),
            pltpu.VMEM((2 * per * cap, units), bf16),
            pltpu.VMEM((experts, cap, width), bf16),
            pltpu.VMEM((experts, cap, width), bf16),
            pltpu.VMEM((experts, cap, width), bf16),
            pltpu.VMEM((experts, cap, width), bf16),
            pltpu.VMEM((experts, cap, width), bf16),
            pltpu.VMEM((row_count, width), f32),
            pltpu.VMEM((row_count, width), f32),
            *(pltpu.VMEM(array.shape, array.dtype) for array in small),
            dma((len(small),)),
            dma((PIECES,)),
            dma((PIECES,)),
            dma((experts,)),
            dma((experts,)),
            dma((experts,)),
            dma((experts,)),
            dma((GROUPS, tiles_two)),
            dma((GROUPS, tiles_two)),
            dma((experts,)),
            dma((experts,)),
        ],
        compiler_params=pltpu.CompilerParams(
            collective_id=0, has_side_effects=True, vmem_limit_bytes=62 * 2**20
        ),
    )(*operands)


def per_device(mesh, *arrays):
    row_count = arrays[0].shape[0]
    experts = mesh.shape["expert"]
    cap = max(2, 4 * row_count // arrays[6].shape[1])
    if mesh.shape["batch"] == 2 and arrays[6].shape[1] == experts and cap == 8 and experts == 16:
        return fused(*arrays)
    return on_device(*arrays)


def solution(mesh):
    return jax.shard_map(
        functools.partial(per_device, mesh),
        mesh=mesh,
        in_specs=(
            P(("batch", "expert"), None),
            P(("batch", "expert"), None),
            P(("batch", "expert"), None, None),
            P(("batch", "expert"), None, None),
            P(("batch", "expert")),
            P(),
            P(),
            P("expert", None, "batch"),
            P("expert", "batch", None),
            P(("batch", "expert"), None),
        ),
        out_specs=P(("batch", "expert"), None),
        check_vma=False,
    )
```
